32 devices in a mesh: attn: 8 (over y, x, core), expert: 4 (over z).
Axes of the slice: x: 2, y: 2, z: 4, core: 2. Of those that a mesh axis runs over, the one named last changes fastest.
Arguments:
- hidden: bfloat16 [4096, 2048], P(('attn', 'expert')), may hold values from -6 to 6
- queries: bfloat16 [4096, 4096], P(('attn', 'expert')), may hold values from -6 to 6
- new_keys: bfloat16 [4096, 512], P(('attn', 'expert')), may hold values from -6 to 6
- new_values: bfloat16 [4096, 512], P(('attn', 'expert')), may hold values from -6 to 6
- cache_keys: bfloat16 [32, 4096, 512], P(('attn', 'expert')), may hold values from -6 to 6
- cache_values: bfloat16 [32, 4096, 512], P(('attn', 'expert')), may hold values from -6 to 6
- option_ids: int32 [32, 128], P(('attn', 'expert')), may hold values from 0 to 3, never falling along the last dimension, each value on 1 to 64 neighbouring positions
- prompt_lengths: int32 [32], P(('attn', 'expert')), may hold values from 1 to 4096, 98304 in all
- query_gain: float32 [128], replicated, may hold values from 0.25 to 1.75
- key_gain: float32 [128], replicated, may hold values from 0.25 to 1.75
- out_proj: bfloat16 [4096, 2048], P('expert'), may hold values from -0.09375 to 0.09375
- post_gain: float32 [2048], replicated, may hold values from 0.25 to 1.75
- route_ids: int32 [4096, 8], P(('attn', 'expert')), may hold values from 0 to 31, all different within a row; in each aligned block of 128 rows (0 to 127, 128 to 255, ...) at most 48 rows name the same one
- route_weights: float32 [4096, 8], P(('attn', 'expert')), may hold values from 0.05 to 1
- expert_gate: bfloat16 [32, 2048, 768], P(('attn', 'expert')), may hold values from -0.125 to 0.125
- expert_up: bfloat16 [32, 2048, 768], P(('attn', 'expert')), may hold values from -0.125 to 0.125
- expert_down: bfloat16 [32, 768, 2048], P(('attn', 'expert')), may hold values from -0.21875 to 0.21875
Outputs:
- layer_out: bfloat16 [4096, 2048], P(('attn', 'expert'))
The draws below stay inside these ranges and needn't reach their ends.
Inputs may be any that keep to these rules, and one draw needn't show every extreme that they name: `route_ids`: each row names 8 different experts. Among the 128 rows of one prompt (an aligned block of rows) no expert is named more than 48 times, and in every draw some expert is named exactly 48 times in some block. `option_ids`: along a prompt's 128 rows the option numbers never fall; each option holds 1 to 64 rows, and some option holds exactly 64. `prompt_lengths`: the lengths of all prompts sum to 98304, and the longest is exactly 4096.
All inputs are finite; a program needn't handle non-finite values. No bound on the sum of `prompt_lengths` on one device may be relied on, other than what follows from the above.
Results may differ from the reference program's by a relative error of at most 0.0095.
Values may be sent and summed in bfloat16 or wider, within the bound.
A program may use at most 128 MiB of HBM per device.

```python
import math
import jax
import jax.numpy as jnp
import numpy as np
from jax import lax

D_MODEL = 2048
HEADS = 32
KV_HEADS = 4
HEAD_DIM = 128
EXPERT_FF = 768
TOP_K = 8
OPTIONS = 4
ANS_DEV = 128
PROMPT_LEN = 4096
EXPERTS = 32
PROMPTS = 32
ROWS = 4096
ANS_MOST = 64
CAPACITY = 48


def levels(own_key, dims, pieces, smallest, high):
    def one(dim, parts):
        draws = jax.random.uniform(jax.random.fold_in(jax.random.fold_in(own_key, 6), dim), (parts,), jnp.float32, smallest / len(pieces), high / len(pieces))
        return jnp.repeat(jnp.exp(draws), dims[dim] // parts).reshape((-1,) + (1,) * (len(dims) - dim - 1))

    level = one(*pieces[0])
    for cut in pieces[1:]:
        level = level * one(*cut)
    return level


def length_profile(number_of, total, bound, slope):
    weights = [(1 << 20) // math.isqrt(grade ** slope) + 1 for grade in range(2, number_of + 1)]
    spare, holding = total - bound - (number_of - 1), [1] * (number_of - 1)
    while spare > 0:
        movable = [i for i in range(number_of - 1) if holding[i] < bound]
        whole, budget = sum([weights[i] for i in movable]), spare
        for i in movable:
            addition = min(bound - holding[i], max(1, budget * weights[i] // whole), spare)
            holding[i] = holding[i] + addition
            spare = spare - addition
    return np.array([bound] + holding)


def ragged(own_key, amount, total, limit, skew):
    if amount == 2:
        one = jax.random.randint(own_key, (), max(1, total - limit), min(limit, total - 1) + 1)
        return jnp.stack([one, total - one])
    lengths = jnp.asarray(length_profile(amount, total, limit, skew), jnp.int32)
    couples = (amount - 1) // 2
    giver, receiver = lengths[1:1 + 2 * couples:2], lengths[2:2 + 2 * couples:2]
    room = jnp.minimum(giver - 1, limit - receiver)
    passed = jax.random.randint(jax.random.fold_in(own_key, 1), (couples,), 0, 1 << 20) % (room + 1)
    lengths = lengths.at[1:1 + 2 * couples:2].set(giver - passed).at[2:2 + 2 * couples:2].set(receiver + passed)
    return lengths[jax.random.permutation(jax.random.fold_in(own_key, 2), amount)]


def shared_out(stream_key, own, number, rows, count, top, most, lean):
    ranking = jax.random.permutation(stream_key, count)
    packed, usual = shares(count, rows * top, most, lean, True), shares(count, rows * top, most, lean, False)
    places = jnp.arange(count)

    def named(lengths, turn):
        used = int((lengths > 0).sum())
        fixed = max(1, used // 4)
        moved = fixed + (places - fixed + turn * (used - fixed)) % max(1, count - fixed)
        return jnp.zeros((count,), jnp.int32).at[ranking[jnp.where(places < fixed, places, moved)]].set(jnp.asarray(lengths, jnp.int32))

    lengths = jnp.where(number % 4 == 0, named(packed, number // 4), named(usual, number - number // 4 - 1))
    mixed = jax.random.permutation(jax.random.fold_in(own, 3), count)
    donor, receiver = mixed[0:count // 2 * 2:2], mixed[1:count // 2 * 2:2]
    margin = jnp.minimum(lengths[donor] - 1, most - lengths[receiver]) // 2
    margin = jnp.where((donor == ranking[0]) | (receiver == ranking[0]) | (lengths[receiver] == 0), 0, jnp.maximum(margin, 0))
    moved = jax.random.randint(jax.random.fold_in(own, 4), (count // 2,), 0, 1 << 20) % (margin + 1)
    lengths = lengths.at[donor].add(-moved).at[receiver].add(moved)
    members = jnp.searchsorted(jnp.cumsum(lengths), jnp.arange(rows * top), side="right").astype(jnp.int32)
    listing = members.reshape(top, rows).T
    listing = listing[jax.random.permutation(jax.random.fold_in(own, 1), rows)]
    turn = jax.random.randint(jax.random.fold_in(own, 2), (rows, 1), 0, top)
    return jnp.take_along_axis(listing, (jnp.arange(top)[None, :] + turn) % top, axis=1)


def shares(number_of, total, bound, slope, full):
    loads = [(1 << 20) // math.isqrt(grade ** slope) + 1 for grade in range(1, number_of + 1)]
    largest = bound if full else min(bound, max(-(-total // number_of), total * loads[0] // sum(loads)))
    least = 1 if total - largest >= number_of - 1 else 0
    counts, rest = [largest] + [least] * (number_of - 1), total - largest - least * (number_of - 1)
    while rest > 0:
        free = [i for i in range(1, number_of) if counts[i] < largest] or [i for i in range(1, number_of) if counts[i] < bound]
        mass, left = sum([loads[i] for i in free]), rest
        for i in free:
            addition = min(bound - counts[i], max(1, left * loads[i] // mass), rest)
            counts[i] = counts[i] + addition
            rest = rest - addition
    return np.array(counts)


def centred(stream_key, shape, spread, most, pieces=(), kind=jnp.bfloat16):
    values = jax.random.normal(stream_key, shape, jnp.float32) * spread
    if len(pieces) > 0:
        values = levels(stream_key, shape, pieces, -0.22, 0.18) * values
    return jnp.clip(values, min=-most, max=most).astype(kind)


def setup_inputs(seed: int = 0) -> dict:
    seeds = jax.random.split(jax.random.key(seed), 18)
    hidden = centred(seeds[0], (ROWS, D_MODEL), 1.0, 6.0, ((0, 32),))
    queries = centred(seeds[1], (ROWS, HEADS * HEAD_DIM), 1.0, 6.0, ((0, 32),))
    new_keys = centred(seeds[2], (ROWS, KV_HEADS * HEAD_DIM), 1.0, 6.0, ((0, 32),))
    new_values = centred(seeds[3], (ROWS, KV_HEADS * HEAD_DIM), 1.0, 6.0, ((0, 32),))
    cache_keys = centred(seeds[4], (PROMPTS, PROMPT_LEN, KV_HEADS * HEAD_DIM), 1.0, 6.0, ((0, 32),))
    cache_values = centred(seeds[5], (PROMPTS, PROMPT_LEN, KV_HEADS * HEAD_DIM), 1.0, 6.0, ((0, 32),))
    option_ids = jax.vmap(lambda own: jnp.searchsorted(jnp.cumsum(ragged(own, OPTIONS, ANS_DEV, ANS_MOST, 1)), jnp.arange(ANS_DEV), side="right"))(jax.random.split(seeds[6], PROMPTS)).reshape((PROMPTS, ANS_DEV)).astype(jnp.int32)
    prompt_lengths = ragged(seeds[7], PROMPTS, 3 * PROMPTS * PROMPT_LEN // 4, PROMPT_LEN, 2).astype(jnp.int32)
    query_gain = jnp.clip(1.0 + 0.15 * jax.random.normal(seeds[8], (HEAD_DIM,), jnp.float32), 0.25, 1.75)
    key_gain = jnp.clip(1.0 + 0.15 * jax.random.normal(seeds[9], (HEAD_DIM,), jnp.float32), 0.25, 1.75)
    out_proj = centred(seeds[10], (HEADS * HEAD_DIM, D_MODEL), (HEADS * HEAD_DIM) ** -0.5, 0.09375, ((0, 4),))
    post_gain = jnp.clip(1.0 + 0.15 * jax.random.normal(seeds[11], (D_MODEL,), jnp.float32), 0.25, 1.75)
    route_ids_keys = jax.random.split(jax.random.fold_in(seeds[12], 1), ROWS // ANS_DEV)
    route_ids_turns = jax.random.permutation(jax.random.fold_in(seeds[12], 3), ROWS // ANS_DEV)
    route_ids = jax.vmap(lambda own, number: shared_out(jax.random.fold_in(seeds[12], 2), own, number, ANS_DEV, EXPERTS, TOP_K, CAPACITY, 2))(route_ids_keys, route_ids_turns).reshape((ROWS, TOP_K))
    route_weights = jnp.clip(jnp.exp(math.log(1.0) - 2.9957323 * jax.random.uniform(seeds[13], (ROWS, TOP_K), jnp.float32) ** levels(seeds[13], (ROWS, TOP_K), ((0, 32),), -0.2, 0.2)), 0.05, 1.0)
    expert_gate = centred(seeds[14], (EXPERTS, D_MODEL, EXPERT_FF), D_MODEL ** -0.5, 0.125, ((0, 32),))
    expert_up = centred(seeds[15], (EXPERTS, D_MODEL, EXPERT_FF), D_MODEL ** -0.5, 0.125, ((0, 32),))
    expert_down = centred(seeds[16], (EXPERTS, EXPERT_FF, D_MODEL), EXPERT_FF ** -0.5, 0.21875, ((0, 32),))
    return {"hidden": hidden, "queries": queries, "new_keys": new_keys, "new_values": new_values, "cache_keys": cache_keys, "cache_values": cache_values, "option_ids": option_ids, "prompt_lengths": prompt_lengths, "query_gain": query_gain, "key_gain": key_gain, "out_proj": out_proj, "post_gain": post_gain, "route_ids": route_ids, "route_weights": route_weights, "expert_gate": expert_gate, "expert_up": expert_up, "expert_down": expert_down}


norm_eps = 1e-06

def rms_scaled(values, gain_row):
    mean_square = lax.optimization_barrier(jnp.mean(values * values, axis=-1, keepdims=True))
    return values * lax.rsqrt(mean_square + norm_eps) * gain_row

def widened_rounded_rows(values):
    return lax.optimization_barrier(values.astype(jnp.bfloat16)).astype(jnp.float32)

def attend_prompt(bundle, query_gain, key_gain):
    query_rows, incoming_keys, fresh_values, past_keys, past_values, option_row, prompt_length = bundle
    groups = HEADS // KV_HEADS
    total_keys = PROMPT_LEN + ANS_DEV
    merged_queries = rms_scaled(query_rows.astype(jnp.float32).reshape(ANS_DEV, KV_HEADS, groups, HEAD_DIM), query_gain)
    merged_queries = widened_rounded_rows(merged_queries * HEAD_DIM ** (-0.5))
    merged_keys = jnp.concatenate([past_keys, incoming_keys], axis=0).astype(jnp.float32).reshape(total_keys, KV_HEADS, HEAD_DIM)
    merged_keys = widened_rounded_rows(rms_scaled(merged_keys, key_gain))
    merged_values = jnp.concatenate([past_values, fresh_values], axis=0).astype(jnp.float32).reshape(total_keys, KV_HEADS, HEAD_DIM)
    logit_scores = jnp.einsum('nfow,pfw->nfop', merged_queries, merged_keys)
    past_live = jnp.arange(PROMPT_LEN, dtype=jnp.int32) < prompt_length
    positions = jnp.arange(ANS_DEV, dtype=jnp.int32)
    fresh_live = (option_row[:, None] == option_row[None, :]) & (positions[None, :] <= positions[:, None])
    visible = jnp.concatenate([jnp.broadcast_to(past_live[None, :], (ANS_DEV, PROMPT_LEN)), fresh_live], axis=1)
    attention_weights = jnp.where(visible[:, None, None, :], jnp.exp(logit_scores), jnp.float32(0.0))
    denominator = lax.optimization_barrier(jnp.sum(attention_weights, axis=-1))
    weighted_values = jnp.einsum('wvof,fvm->wvom', widened_rounded_rows(attention_weights), merged_values)
    return (weighted_values / denominator[..., None]).reshape(ANS_DEV, HEADS * HEAD_DIM).astype(jnp.bfloat16)

def rank_block(id_block):
    onehot = (id_block[:, None] == jnp.arange(EXPERTS, dtype=jnp.int32)[None, :]).astype(jnp.int32)
    earlier = jnp.cumsum(onehot, axis=0) - onehot
    return lax.optimization_barrier(jnp.sum(earlier * onehot, axis=1)).astype(jnp.int32)

def reference(hidden, queries, new_keys, new_values, cache_keys, cache_values, option_ids, prompt_lengths, query_gain, key_gain, out_proj, post_gain, route_ids, route_weights, expert_gate, expert_up, expert_down):

    def one_prompt(bundle):
        return attend_prompt(bundle, query_gain, key_gain)
    attended = lax.map(one_prompt, (queries.reshape(PROMPTS, ANS_DEV, HEADS * HEAD_DIM), new_keys.reshape(PROMPTS, ANS_DEV, KV_HEADS * HEAD_DIM), new_values.reshape(PROMPTS, ANS_DEV, KV_HEADS * HEAD_DIM), cache_keys, cache_values, option_ids, prompt_lengths))
    attended = attended.reshape(ROWS, HEADS * HEAD_DIM)
    projected = jnp.dot(attended, out_proj, preferred_element_type=jnp.float32)
    residual = (hidden.astype(jnp.float32) + projected).astype(jnp.bfloat16)
    normed = rms_scaled(residual.astype(jnp.float32), post_gain).astype(jnp.bfloat16)
    gate_share = route_weights / lax.optimization_barrier(jnp.sum(route_weights, axis=1, keepdims=True))
    sources = ROWS // ANS_DEV
    slot_rank = lax.map(rank_block, route_ids.reshape(sources, ANS_DEV * TOP_K)).reshape(ROWS * TOP_K)
    route_flat = route_ids.reshape(ROWS * TOP_K)
    entries = jnp.arange(ROWS * TOP_K, dtype=jnp.int32)
    row_owner = entries // TOP_K
    source_owner = entries // (ANS_DEV * TOP_K)
    expert_span = sources * CAPACITY
    position = route_flat * expert_span + source_owner * CAPACITY + slot_rank
    table_rows = jnp.full((EXPERTS * expert_span,), ROWS, dtype=jnp.int32).at[position].set(row_owner).reshape(EXPERTS, expert_span)
    table_gates = jnp.zeros((EXPERTS * expert_span,), dtype=jnp.float32).at[position].set(gate_share.reshape(ROWS * TOP_K)).reshape(EXPERTS, expert_span)
    padded = jnp.concatenate([normed, jnp.zeros((1, D_MODEL), dtype=jnp.bfloat16)], axis=0)

    def expert_step(accumulated, bundle):
        gate_matrix, up_matrix, down_matrix, row_index, gate_value = bundle
        inputs = padded[row_index]
        gate_part = jnp.dot(inputs, gate_matrix, preferred_element_type=jnp.float32)
        up_part = jnp.dot(inputs, up_matrix, preferred_element_type=jnp.float32)
        activated = (jax.nn.silu(gate_part) * up_part).astype(jnp.bfloat16)
        output = jnp.dot(activated, down_matrix, preferred_element_type=jnp.float32).astype(jnp.bfloat16)
        accumulated = accumulated.at[row_index].add(gate_value[:, None] * output.astype(jnp.float32))
        return (accumulated, gate_value[0])
    mixture = lax.scan(expert_step, jnp.zeros((ROWS + 1, D_MODEL), dtype=jnp.float32), (expert_gate, expert_up, expert_down, table_rows, table_gates))[0]
    return (residual.astype(jnp.float32) + mixture[:ROWS]).astype(jnp.bfloat16)
```

```python
import functools

import jax
import jax.numpy as jnp
from jax import lax
from jax.experimental import pallas as pl
from jax.experimental.pallas import tpu as pltpu
from jax.sharding import PartitionSpec as P

norm_eps = 1e-06
log2_e = 1.4426950408889634


def rms_scaled(values, gain_row):
    mean_square = jnp.mean(values * values, axis=-1, keepdims=True)
    return values * lax.rsqrt(mean_square + norm_eps) * gain_row


def attention_kernel(
    key_block,
    length_ref,
    query_ref,
    new_key_ref,
    new_value_ref,
    past_key_ref,
    past_value_ref,
    option_row_ref,
    option_column_ref,
    query_gain_ref,
    key_gain_ref,
    out_ref,
    query_unit,
    total,
):
    head_dim = query_gain_ref.shape[1]
    answer_rows = query_ref.shape[0]
    groups = query_ref.shape[1] // head_dim
    query_gain = query_gain_ref[...] * (head_dim ** (-0.5) * log2_e)
    key_gain = key_gain_ref[...]
    for group in range(groups):
        rows = query_ref[:, group * head_dim : (group + 1) * head_dim].astype(jnp.float32)
        query_unit[group * answer_rows : (group + 1) * answer_rows, :] = rms_scaled(
            rows, query_gain
        ).astype(jnp.bfloat16)

    def block_sum(keys, values, visible):
        keys = rms_scaled(keys.astype(jnp.float32), key_gain).astype(jnp.bfloat16)
        scores = lax.dot_general(
            query_unit[...], keys, (((1,), (1,)), ((), ())), preferred_element_type=jnp.float32
        )
        weights = jnp.exp2(scores)
        if visible is not None:
            weights = jnp.where(visible, weights, 0.0)
        wide = jnp.concatenate([values, jnp.ones_like(values)], axis=1)
        return jnp.dot(weights.astype(jnp.bfloat16), wide, preferred_element_type=jnp.float32)

    position_row = lax.broadcasted_iota(jnp.int32, (answer_rows, answer_rows), 0)
    position_column = lax.broadcasted_iota(jnp.int32, (answer_rows, answer_rows), 1)
    fresh = ((option_column_ref[...] == option_row_ref[...]) & (position_column <= position_row)).astype(
        jnp.float32
    )
    fresh = jnp.concatenate([fresh] * groups, axis=0) > 0.5
    total[...] = block_sum(new_key_ref[...], new_value_ref[...], fresh)
    length = length_ref[0]
    whole = length // key_block

    @pl.loop(0, whole)
    def _(index):
        here = pl.ds(pl.multiple_of(index * key_block, key_block), key_block)
        total[...] += block_sum(past_key_ref[here, :], past_value_ref[here, :], None)

    @pl.when(whole * key_block < length)
    def _():
        first = pl.multiple_of(whole * key_block, key_block)
        here = pl.ds(first, key_block)
        visible = first + lax.broadcasted_iota(jnp.int32, (1, key_block), 1) < length
        total[...] += block_sum(past_key_ref[here, :], past_value_ref[here, :], visible)

    for group in range(groups):
        rows = slice(group * answer_rows, (group + 1) * answer_rows)
        out_ref[:, group * head_dim : (group + 1) * head_dim] = (
            total[rows, :head_dim] / total[rows, head_dim:]
        ).astype(jnp.bfloat16)


def attend(
    queries,
    new_keys,
    new_values,
    past_keys,
    past_values,
    option_ids,
    length,
    query_gain,
    key_gain,
):
    answer_rows = queries.shape[0]
    head_dim = query_gain.shape[0]
    prompt_len = past_keys.shape[0]
    key_heads = new_keys.shape[1] // head_dim
    group_width = queries.shape[1] // key_heads
    groups = group_width // head_dim
    key_block = min(512, prompt_len)

    def by_head(rows, width):
        return pl.BlockSpec((rows, width), lambda head, length: (0, head))

    def fixed(rows, width):
        return pl.BlockSpec((rows, width), lambda head, length: (0, 0))

    return pl.pallas_call(
        functools.partial(attention_kernel, key_block),
        out_shape=jax.ShapeDtypeStruct(queries.shape, jnp.bfloat16),
        grid_spec=pltpu.PrefetchScalarGridSpec(
            num_scalar_prefetch=1,
            grid=(key_heads,),
            in_specs=[
                by_head(answer_rows, group_width),
                by_head(answer_rows, head_dim),
                by_head(answer_rows, head_dim),
                by_head(prompt_len, head_dim),
                by_head(prompt_len, head_dim),
                fixed(1, answer_rows),
                fixed(answer_rows, 1),
                fixed(1, head_dim),
                fixed(1, head_dim),
            ],
            out_specs=by_head(answer_rows, group_width),
            scratch_shapes=[
                pltpu.VMEM((groups * answer_rows, head_dim), jnp.bfloat16),
                pltpu.VMEM((groups * answer_rows, 2 * head_dim), jnp.float32),
            ],
        ),
        compiler_params=pltpu.CompilerParams(vmem_limit_bytes=32 * 2**20),
        cost_estimate=pl.CostEstimate(
            flops=4 * queries.size * prompt_len,
            bytes_accessed=4 * past_keys.size,
            transcendentals=queries.size // head_dim * prompt_len,
        ),
        name="attend",
    )(
        length,
        queries,
        new_keys,
        new_values,
        past_keys,
        past_values,
        option_ids,
        option_ids.reshape(answer_rows, 1),
        query_gain.reshape(1, head_dim),
        key_gain.reshape(1, head_dim),
    )


def on_device(
    hidden,
    queries,
    new_keys,
    new_values,
    cache_keys,
    cache_values,
    option_ids,
    prompt_lengths,
    query_gain,
    key_gain,
    out_proj,
    post_gain,
    route_ids,
    route_weights,
    expert_gate,
    expert_up,
    expert_down,
):
    answer_rows, model_width = hidden.shape
    top_count = route_ids.shape[1]
    attn_count = lax.axis_size("attn")
    expert_count = lax.axis_size("expert")
    device_count = attn_count * expert_count
    capacity = 3 * answer_rows * top_count // (2 * device_count)
    capacity = (capacity + 15) // 16 * 16
    plane = lax.axis_index("expert")

    gate_share = route_weights / jnp.sum(route_weights, axis=1, keepdims=True)
    ids = lax.all_gather(route_ids, "expert")
    shares = lax.all_gather(gate_share, "expert")
    plane_experts = jnp.arange(attn_count, dtype=jnp.int32) * expert_count + plane
    chosen = ids[:, None, :, :] == plane_experts[None, :, None, None]
    share = jnp.sum(jnp.where(chosen, shares[:, None, :, :], 0.0), axis=-1)
    hit = jnp.any(chosen, axis=-1)
    earlier = (
        jnp.arange(answer_rows)[:, None] < jnp.arange(answer_rows)[None, :]
    ).astype(jnp.bfloat16)
    rank = jnp.einsum(
        "ear,rs->eas", hit.astype(jnp.bfloat16), earlier, preferred_element_type=jnp.float32
    ).astype(jnp.int32)
    slot = jnp.where(hit, rank, -1)
    picks = slot[:, :, None, :] == jnp.arange(capacity, dtype=jnp.int32)[None, None, :, None]
    select = picks.astype(jnp.bfloat16)
    combine = jnp.where(picks, share[:, :, None, :], 0.0).astype(jnp.bfloat16)

    attended = attend(
        queries,
        new_keys,
        new_values,
        cache_keys[0],
        cache_values[0],
        option_ids,
        prompt_lengths,
        query_gain,
        key_gain,
    )
    swapped = lax.all_to_all(attended, "expert", split_axis=1, concat_axis=0, tiled=True)
    projected = lax.psum_scatter(
        jnp.dot(swapped, out_proj, preferred_element_type=jnp.float32).astype(jnp.bfloat16),
        "expert",
        scatter_dimension=0,
        tiled=True,
    ).astype(jnp.float32)
    residual = (hidden.astype(jnp.float32) + projected).astype(jnp.bfloat16)
    normed = rms_scaled(residual.astype(jnp.float32), post_gain).astype(jnp.bfloat16)

    column = lax.all_gather(normed, "expert")
    outgoing = jnp.einsum(
        "eacr,erd->aecd", select, column, preferred_element_type=jnp.float32
    ).astype(jnp.bfloat16)
    arrived = lax.all_to_all(outgoing, "attn", split_axis=0, concat_axis=0, tiled=True)
    flat_rows = arrived.reshape(-1, model_width)
    gate_part = jnp.dot(flat_rows, expert_gate[0], preferred_element_type=jnp.float32)
    up_part = jnp.dot(flat_rows, expert_up[0], preferred_element_type=jnp.float32)
    activated = (jax.nn.silu(gate_part) * up_part).astype(jnp.bfloat16)
    returned = lax.all_to_all(
        jnp.dot(activated, expert_down[0], preferred_element_type=jnp.float32)
        .astype(jnp.bfloat16)
        .reshape(arrived.shape),
        "attn",
        split_axis=0,
        concat_axis=0,
        tiled=True,
    )
    partial = jnp.einsum(
        "eacr,aecd->erd", combine, returned, preferred_element_type=jnp.float32
    ).astype(jnp.bfloat16)
    mixture = lax.psum_scatter(partial, "expert", scatter_dimension=0, tiled=True)[0]
    return (residual.astype(jnp.float32) + mixture.astype(jnp.float32)).astype(jnp.bfloat16)


def solution(mesh):
    rows = P(("attn", "expert"), None)
    blocks = P(("attn", "expert"), None, None)
    placed = (
        rows,
        rows,
        rows,
        rows,
        blocks,
        blocks,
        rows,
        P(("attn", "expert")),
        P(),
        P(),
        P("expert", None),
        P(),
        rows,
        rows,
        blocks,
        blocks,
        blocks,
    )
    return jax.shard_map(
        on_device,
        mesh=mesh,
        in_specs=placed,
        out_specs=rows,
        check_vma=False,
    )
```

```python
import functools

import jax
import jax.numpy as jnp
from jax import lax
from jax.experimental import pallas as pl
from jax.experimental.pallas import tpu as pltpu
from jax.sharding import PartitionSpec as P

norm_eps = 1e-06
log2_e = 1.4426950408889634


def rms_scaled(values, gain_row):
    mean_square = jnp.mean(values * values, axis=-1, keepdims=True)
    return values * lax.rsqrt(mean_square + norm_eps) * gain_row


def attention_kernel(
    key_block,
    length_ref,
    query_ref,
    new_key_ref,
    new_value_ref,
    past_key_ref,
    past_value_ref,
    option_row_ref,
    option_column_ref,
    query_gain_ref,
    key_gain_ref,
    out_ref,
    query_unit,
    total,
):
    head_dim = query_gain_ref.shape[1]
    answer_rows = query_ref.shape[0]
    groups = query_ref.shape[1] // head_dim
    query_gain = query_gain_ref[...] * (head_dim ** (-0.5) * log2_e)
    key_gain = key_gain_ref[...]
    for group in range(groups):
        rows = query_ref[:, group * head_dim : (group + 1) * head_dim].astype(jnp.float32)
        query_unit[group * answer_rows : (group + 1) * answer_rows, :] = rms_scaled(
            rows, query_gain
        ).astype(jnp.bfloat16)

    def block_sum(keys, values, visible):
        keys = rms_scaled(keys.astype(jnp.float32), key_gain).astype(jnp.bfloat16)
        scores = lax.dot_general(
            query_unit[...], keys, (((1,), (1,)), ((), ())), preferred_element_type=jnp.float32
        )
        weights = jnp.exp2(scores)
        if visible is not None:
            weights = jnp.where(visible, weights, 0.0)
        wide = jnp.concatenate([values, jnp.ones_like(values)], axis=1)
        return jnp.dot(weights.astype(jnp.bfloat16), wide, preferred_element_type=jnp.float32)

    position_row = lax.broadcasted_iota(jnp.int32, (answer_rows, answer_rows), 0)
    position_column = lax.broadcasted_iota(jnp.int32, (answer_rows, answer_rows), 1)
    fresh = ((option_column_ref[...] == option_row_ref[...]) & (position_column <= position_row)).astype(
        jnp.float32
    )
    fresh = jnp.concatenate([fresh] * groups, axis=0) > 0.5
    total[...] = block_sum(new_key_ref[...], new_value_ref[...], fresh)
    length = length_ref[0]
    whole = length // key_block

    @pl.loop(0, whole)
    def _(index):
        here = pl.ds(pl.multiple_of(index * key_block, key_block), key_block)
        total[...] += block_sum(past_key_ref[here, :], past_value_ref[here, :], None)

    @pl.when(whole * key_block < length)
    def _():
        first = pl.multiple_of(whole * key_block, key_block)
        here = pl.ds(first, key_block)
        visible = first + lax.broadcasted_iota(jnp.int32, (1, key_block), 1) < length
        total[...] += block_sum(past_key_ref[here, :], past_value_ref[here, :], visible)

    for group in range(groups):
        rows = slice(group * answer_rows, (group + 1) * answer_rows)
        out_ref[:, group * head_dim : (group + 1) * head_dim] = (
            total[rows, :head_dim] / total[rows, head_dim:]
        ).astype(jnp.bfloat16)


def attend(
    queries,
    new_keys,
    new_values,
    past_keys,
    past_values,
    option_ids,
    length,
    query_gain,
    key_gain,
):
    answer_rows = queries.shape[0]
    head_dim = query_gain.shape[0]
    prompt_len = past_keys.shape[0]
    key_heads = new_keys.shape[1] // head_dim
    group_width = queries.shape[1] // key_heads
    groups = group_width // head_dim
    key_block = min(512, prompt_len)

    def by_head(rows, width):
        return pl.BlockSpec((rows, width), lambda head, length: (0, head))

    def fixed(rows, width):
        return pl.BlockSpec((rows, width), lambda head, length: (0, 0))

    return pl.pallas_call(
        functools.partial(attention_kernel, key_block),
        out_shape=jax.ShapeDtypeStruct(queries.shape, jnp.bfloat16),
        grid_spec=pltpu.PrefetchScalarGridSpec(
            num_scalar_prefetch=1,
            grid=(key_heads,),
            in_specs=[
                by_head(answer_rows, group_width),
                by_head(answer_rows, head_dim),
                by_head(answer_rows, head_dim),
                by_head(prompt_len, head_dim),
                by_head(prompt_len, head_dim),
                fixed(1, answer_rows),
                fixed(answer_rows, 1),
                fixed(1, head_dim),
                fixed(1, head_dim),
            ],
            out_specs=by_head(answer_rows, group_width),
            scratch_shapes=[
                pltpu.VMEM((groups * answer_rows, head_dim), jnp.bfloat16),
                pltpu.VMEM((groups * answer_rows, 2 * head_dim), jnp.float32),
            ],
        ),
        compiler_params=pltpu.CompilerParams(vmem_limit_bytes=32 * 2**20),
        cost_estimate=pl.CostEstimate(
            flops=4 * queries.size * prompt_len,
            bytes_accessed=4 * past_keys.size,
            transcendentals=queries.size // head_dim * prompt_len,
        ),
        name="attend",
    )(
        length,
        queries,
        new_keys,
        new_values,
        past_keys,
        past_values,
        option_ids,
        option_ids.reshape(answer_rows, 1),
        query_gain.reshape(1, head_dim),
        key_gain.reshape(1, head_dim),
    )


def experts_kernel(
    residual_ref,
    normed_ref,
    select_ref,
    combine_ref,
    gate_ref,
    up_ref,
    down_ref,
    out_ref,
    column,
    outbox,
    inbox,
    returned,
    partial,
    summed,
    column_send,
    column_recv,
    out_send,
    out_recv,
    back_send,
    back_recv,
    sum_send,
    sum_recv,
):
    planes, places, capacity, model_width = inbox.shape
    me = lax.axis_index("attn")
    plane = lax.axis_index("expert")

    def other_plane(step):
        return lax.rem(plane + step, planes)

    def other_place(step):
        return lax.rem(me + step, places)

    def column_copy(source, target, owner):
        return pltpu.make_async_remote_copy(
            src_ref=normed_ref,
            dst_ref=column.at[owner],
            send_sem=column_send.at[target],
            recv_sem=column_recv.at[owner],
            device_id=(me, source),
            device_id_type=pl.DeviceIdType.MESH,
        )

    def out_copy(block, target, owner):
        return pltpu.make_async_remote_copy(
            src_ref=outbox.at[block, target],
            dst_ref=inbox.at[block, owner],
            send_sem=out_send.at[block, target],
            recv_sem=out_recv.at[block, owner],
            device_id=(target, plane),
            device_id_type=pl.DeviceIdType.MESH,
        )

    def back_copy(block, target, owner):
        return pltpu.make_async_remote_copy(
            src_ref=inbox.at[block, target],
            dst_ref=returned.at[block, owner],
            send_sem=back_send.at[block, target],
            recv_sem=back_recv.at[block, owner],
            device_id=(target, plane),
            device_id_type=pl.DeviceIdType.MESH,
        )

    def sum_copy(target, owner):
        return pltpu.make_async_remote_copy(
            src_ref=partial.at[target],
            dst_ref=summed.at[owner],
            send_sem=sum_send.at[target],
            recv_sem=sum_recv.at[owner],
            device_id=(me, target),
            device_id_type=pl.DeviceIdType.MESH,
        )

    barrier = pltpu.get_barrier_semaphore()

    @pl.loop(1, planes)
    def _(step):
        pl.semaphore_signal(
            barrier,
            inc=1,
            device_id=(me, other_plane(step)),
            device_id_type=pl.DeviceIdType.MESH,
        )

    @pl.loop(1, places)
    def _(step):
        pl.semaphore_signal(
            barrier,
            inc=1,
            device_id=(other_place(step), plane),
            device_id_type=pl.DeviceIdType.MESH,
        )

    pl.semaphore_wait(barrier, planes + places - 2)

    @pl.loop(1, planes)
    def _(step):
        target = other_plane(step)
        column_copy(target, target, plane).start()

    column[plane] = normed_ref[...]

    def dispatch(block):
        def rows_for(place):
            return jnp.dot(
                select_ref[block, place], column[block], preferred_element_type=jnp.float32
            ).astype(jnp.bfloat16)

        @pl.loop(1, places)
        def _(step):
            target = other_place(step)
            outbox[block, target] = rows_for(target)
            out_copy(block, target, me).start()

        inbox[block, me] = rows_for(me)

    dispatch(plane)

    @pl.loop(1, planes)
    def _(step):
        block = other_plane(planes - step)
        column_copy(block, block, block).wait_recv()
        dispatch(block)

    @pl.loop(1, planes + 1)
    def _(step):
        block = other_plane(planes - lax.rem(step, planes))

        @pl.loop(1, places)
        def _(turn):
            owner = other_place(turn)
            out_copy(block, owner, owner).wait_recv()

        rows = inbox[block].reshape(places * capacity, model_width)
        gate_part = jnp.dot(rows, gate_ref[...], preferred_element_type=jnp.float32)
        up_part = jnp.dot(rows, up_ref[...], preferred_element_type=jnp.float32)
        activated = (gate_part / (1.0 + jnp.exp(-gate_part)) * up_part).astype(jnp.bfloat16)
        inbox[block] = (
            jnp.dot(activated, down_ref[...], preferred_element_type=jnp.float32)
            .astype(jnp.bfloat16)
            .reshape(places, capacity, model_width)
        )

        @pl.loop(1, places)
        def _(turn):
            back_copy(block, other_place(turn), me).start()

        returned[block, me] = inbox[block, me]

    def combined(block):
        @pl.loop(1, places)
        def _(turn):
            owner = other_place(turn)
            back_copy(block, owner, owner).wait_recv()

        return jnp.dot(
            combine_ref[block],
            returned[block].reshape(places * capacity, model_width),
            preferred_element_type=jnp.float32,
        )

    @pl.loop(1, planes)
    def _(step):
        block = other_plane(planes - step)
        partial[block] = combined(block).astype(jnp.bfloat16)
        sum_copy(block, plane).start()

    total = residual_ref[...].astype(jnp.float32) + combined(plane)
    for step in range(1, planes):
        owner = other_plane(step)
        sum_copy(owner, owner).wait_recv()
        total = total + summed[owner].astype(jnp.float32)
    out_ref[...] = total.astype(jnp.bfloat16)

    @pl.loop(1, planes)
    def _(step):
        target = other_plane(step)
        column_copy(target, target, plane).wait_send()
        sum_copy(target, plane).wait_send()

    @pl.loop(0, planes)
    def _(block):
        @pl.loop(1, places)
        def _(turn):
            target = other_place(turn)
            out_copy(block, target, me).wait_send()
            back_copy(block, target, me).wait_send()


def mix_experts(residual, normed, select, combine, gate_matrix, up_matrix, down_matrix):
    planes, places, capacity, answer_rows = select.shape
    model_width = normed.shape[1]
    box = pltpu.VMEM((planes, places, capacity, model_width), jnp.bfloat16)
    blocks = pltpu.VMEM((planes, answer_rows, model_width), jnp.bfloat16)
    per_plane = pltpu.SemaphoreType.DMA((planes,))
    per_pair = pltpu.SemaphoreType.DMA((planes, places))
    return pl.pallas_call(
        experts_kernel,
        out_shape=jax.ShapeDtypeStruct(residual.shape, jnp.bfloat16),
        in_specs=[pl.BlockSpec(memory_space=pltpu.VMEM)] * 7,
        out_specs=pl.BlockSpec(memory_space=pltpu.VMEM),
        scratch_shapes=[box_shape for box_shape in (blocks, box, box, box, blocks, blocks)]
        + [per_plane, per_plane, per_pair, per_pair, per_pair, per_pair, per_plane, per_plane],
        compiler_params=pltpu.CompilerParams(
            collective_id=0, has_side_effects=True, vmem_limit_bytes=60 * 2**20
        ),
        cost_estimate=pl.CostEstimate(
            flops=6 * planes * places * capacity * gate_matrix.size,
            bytes_accessed=6 * gate_matrix.size,
            transcendentals=0,
        ),
        name="mix_experts",
    )(residual, normed, select, combine, gate_matrix, up_matrix, down_matrix)


def on_device(
    hidden,
    queries,
    new_keys,
    new_values,
    cache_keys,
    cache_values,
    option_ids,
    prompt_lengths,
    query_gain,
    key_gain,
    out_proj,
    post_gain,
    route_ids,
    route_weights,
    expert_gate,
    expert_up,
    expert_down,
):
    answer_rows, model_width = hidden.shape
    top_count = route_ids.shape[1]
    attn_count = lax.axis_size("attn")
    expert_count = lax.axis_size("expert")
    device_count = attn_count * expert_count
    capacity = 3 * answer_rows * top_count // (2 * device_count)
    capacity = (capacity + 15) // 16 * 16
    plane = lax.axis_index("expert")

    gate_share = route_weights / jnp.sum(route_weights, axis=1, keepdims=True)
    ids = lax.all_gather(route_ids, "expert")
    shares = lax.all_gather(gate_share, "expert")
    plane_experts = jnp.arange(attn_count, dtype=jnp.int32) * expert_count + plane
    chosen = ids[:, None, :, :] == plane_experts[None, :, None, None]
    share = jnp.sum(jnp.where(chosen, shares[:, None, :, :], 0.0), axis=-1)
    hit = jnp.any(chosen, axis=-1)
    earlier = (
        jnp.arange(answer_rows)[:, None] < jnp.arange(answer_rows)[None, :]
    ).astype(jnp.bfloat16)
    rank = jnp.einsum(
        "ear,rs->eas", hit.astype(jnp.bfloat16), earlier, preferred_element_type=jnp.float32
    ).astype(jnp.int32)
    slot = jnp.where(hit, rank, -1)
    picks = slot[:, :, None, :] == jnp.arange(capacity, dtype=jnp.int32)[None, None, :, None]
    select = picks.astype(jnp.bfloat16)
    combine = jnp.where(picks, share[:, :, None, :], 0.0).astype(jnp.bfloat16)

    attended = attend(
        queries,
        new_keys,
        new_values,
        cache_keys[0],
        cache_values[0],
        option_ids,
        prompt_lengths,
        query_gain,
        key_gain,
    )
    swapped = lax.all_to_all(attended, "expert", split_axis=1, concat_axis=0, tiled=True)
    projected = lax.psum_scatter(
        jnp.dot(swapped, out_proj, preferred_element_type=jnp.float32).astype(jnp.bfloat16),
        "expert",
        scatter_dimension=0,
        tiled=True,
    ).astype(jnp.float32)
    residual = (hidden.astype(jnp.float32) + projected).astype(jnp.bfloat16)
    normed = rms_scaled(residual.astype(jnp.float32), post_gain).astype(jnp.bfloat16)

    combine = combine.transpose(0, 3, 1, 2).reshape(
        expert_count, answer_rows, attn_count * capacity
    )
    return mix_experts(
        residual,
        normed,
        select,
        combine,
        expert_gate[0],
        expert_up[0],
        expert_down[0],
    )


def solution(mesh):
    rows = P(("attn", "expert"), None)
    blocks = P(("attn", "expert"), None, None)
    placed = (
        rows,
        rows,
        rows,
        rows,
        blocks,
        blocks,
        rows,
        P(("attn", "expert")),
        P(),
        P(),
        P("expert", None),
        P(),
        rows,
        rows,
        blocks,
        blocks,
        blocks,
    )
    return jax.shard_map(
        on_device,
        mesh=mesh,
        in_specs=placed,
        out_specs=rows,
        check_vma=False,
    )
```

```python
import functools

import jax
import jax.numpy as jnp
from jax import lax
from jax.experimental import pallas as pl
from jax.experimental.pallas import tpu as pltpu
from jax.sharding import PartitionSpec as P

norm_eps = 1e-06
log2_e = 1.4426950408889634


def rms_scaled(values, gain_row):
    mean_square = jnp.mean(values * values, axis=-1, keepdims=True)
    return values * lax.rsqrt(mean_square + norm_eps) * gain_row


def attention_kernel(
    key_block,
    length_ref,
    query_ref,
    new_key_ref,
    new_value_ref,
    past_key_ref,
    past_value_ref,
    option_row_ref,
    option_column_ref,
    query_gain_ref,
    key_gain_ref,
    out_ref,
    query_unit,
    total,
):
    head_dim = query_gain_ref.shape[1]
    answer_rows = query_ref.shape[0]
    groups = query_ref.shape[1] // head_dim
    query_gain = query_gain_ref[...] * (head_dim ** (-0.5) * log2_e)
    key_gain = key_gain_ref[...]
    for group in range(groups):
        rows = query_ref[:, group * head_dim : (group + 1) * head_dim].astype(jnp.float32)
        query_unit[group * answer_rows : (group + 1) * answer_rows, :] = rms_scaled(
            rows, query_gain
        ).astype(jnp.bfloat16)

    def block_sum(keys, values, visible):
        keys = rms_scaled(keys.astype(jnp.float32), key_gain).astype(jnp.bfloat16)
        scores = lax.dot_general(
            query_unit[...], keys, (((1,), (1,)), ((), ())), preferred_element_type=jnp.float32
        )
        weights = jnp.exp2(scores)
        if visible is not None:
            weights = jnp.where(visible, weights, 0.0)
        wide = jnp.concatenate([values, jnp.ones_like(values)], axis=1)
        return jnp.dot(weights.astype(jnp.bfloat16), wide, preferred_element_type=jnp.float32)

    position_row = lax.broadcasted_iota(jnp.int32, (answer_rows, answer_rows), 0)
    position_column = lax.broadcasted_iota(jnp.int32, (answer_rows, answer_rows), 1)
    fresh = ((option_column_ref[...] == option_row_ref[...]) & (position_column <= position_row)).astype(
        jnp.float32
    )
    fresh = jnp.concatenate([fresh] * groups, axis=0) > 0.5
    total[...] = block_sum(new_key_ref[...], new_value_ref[...], fresh)
    length = length_ref[0]
    whole = length // key_block

    @pl.loop(0, whole)
    def _(index):
        here = pl.ds(pl.multiple_of(index * key_block, key_block), key_block)
        total[...] += block_sum(past_key_ref[here, :], past_value_ref[here, :], None)

    @pl.when(whole * key_block < length)
    def _():
        first = pl.multiple_of(whole * key_block, key_block)
        here = pl.ds(first, key_block)
        visible = first + lax.broadcasted_iota(jnp.int32, (1, key_block), 1) < length
        total[...] += block_sum(past_key_ref[here, :], past_value_ref[here, :], visible)

    for group in range(groups):
        rows = slice(group * answer_rows, (group + 1) * answer_rows)
        out_ref[:, group * head_dim : (group + 1) * head_dim] = (
            total[rows, :head_dim] / total[rows, head_dim:]
        ).astype(jnp.bfloat16)


def attend(
    queries,
    new_keys,
    new_values,
    past_keys,
    past_values,
    option_ids,
    length,
    query_gain,
    key_gain,
):
    answer_rows = queries.shape[0]
    head_dim = query_gain.shape[0]
    prompt_len = past_keys.shape[0]
    key_heads = new_keys.shape[1] // head_dim
    group_width = queries.shape[1] // key_heads
    groups = group_width // head_dim
    key_block = min(512, prompt_len)

    def by_head(rows, width):
        return pl.BlockSpec((rows, width), lambda head, length: (0, head))

    def fixed(rows, width):
        return pl.BlockSpec((rows, width), lambda head, length: (0, 0))

    return pl.pallas_call(
        functools.partial(attention_kernel, key_block),
        out_shape=jax.ShapeDtypeStruct(queries.shape, jnp.bfloat16),
        grid_spec=pltpu.PrefetchScalarGridSpec(
            num_scalar_prefetch=1,
            grid=(key_heads,),
            in_specs=[
                by_head(answer_rows, group_width),
                by_head(answer_rows, head_dim),
                by_head(answer_rows, head_dim),
                by_head(prompt_len, head_dim),
                by_head(prompt_len, head_dim),
                fixed(1, answer_rows),
                fixed(answer_rows, 1),
                fixed(1, head_dim),
                fixed(1, head_dim),
            ],
            out_specs=by_head(answer_rows, group_width),
            scratch_shapes=[
                pltpu.VMEM((groups * answer_rows, head_dim), jnp.bfloat16),
                pltpu.VMEM((groups * answer_rows, 2 * head_dim), jnp.float32),
            ],
        ),
        compiler_params=pltpu.CompilerParams(vmem_limit_bytes=32 * 2**20),
        cost_estimate=pl.CostEstimate(
            flops=4 * queries.size * prompt_len,
            bytes_accessed=4 * past_keys.size,
            transcendentals=queries.size // head_dim * prompt_len,
        ),
        name="attend",
    )(
        length,
        queries,
        new_keys,
        new_values,
        past_keys,
        past_values,
        option_ids,
        option_ids.reshape(answer_rows, 1),
        query_gain.reshape(1, head_dim),
        key_gain.reshape(1, head_dim),
    )


def experts_kernel(
    residual_ref,
    normed_ref,
    routing_ref,
    gate_ref,
    up_ref,
    down_ref,
    out_ref,
    routing,
    column,
    outbox,
    inbox,
    returned,
    partial,
    summed,
    routing_send,
    routing_recv,
    column_send,
    column_recv,
    out_send,
    out_recv,
    back_send,
    back_recv,
    sum_send,
    sum_recv,
):
    planes, places, capacity, model_width = inbox.shape
    me = lax.axis_index("attn")
    plane = lax.axis_index("expert")

    def other_plane(step):
        return lax.rem(plane + step, planes)

    def other_place(step):
        return lax.rem(me + step, places)

    def routing_copy(target, owner):
        return pltpu.make_async_remote_copy(
            src_ref=routing_ref.at[target],
            dst_ref=routing.at[owner],
            send_sem=routing_send.at[target],
            recv_sem=routing_recv.at[owner],
            device_id=(me, target),
            device_id_type=pl.DeviceIdType.MESH,
        )

    def column_copy(source, target, owner):
        return pltpu.make_async_remote_copy(
            src_ref=normed_ref,
            dst_ref=column.at[owner],
            send_sem=column_send.at[target],
            recv_sem=column_recv.at[owner],
            device_id=(me, source),
            device_id_type=pl.DeviceIdType.MESH,
        )

    def out_copy(block, target, owner):
        return pltpu.make_async_remote_copy(
            src_ref=outbox.at[block, target],
            dst_ref=inbox.at[block, owner],
            send_sem=out_send.at[block, target],
            recv_sem=out_recv.at[block, owner],
            device_id=(target, plane),
            device_id_type=pl.DeviceIdType.MESH,
        )

    def back_copy(block, target, owner):
        return pltpu.make_async_remote_copy(
            src_ref=inbox.at[block, target],
            dst_ref=returned.at[block, owner],
            send_sem=back_send.at[block, target],
            recv_sem=back_recv.at[block, owner],
            device_id=(target, plane),
            device_id_type=pl.DeviceIdType.MESH,
        )

    def sum_copy(target, owner):
        return pltpu.make_async_remote_copy(
            src_ref=partial.at[target],
            dst_ref=summed.at[owner],
            send_sem=sum_send.at[target],
            recv_sem=sum_recv.at[owner],
            device_id=(me, target),
            device_id_type=pl.DeviceIdType.MESH,
        )

    barrier = pltpu.get_barrier_semaphore()

    @pl.loop(1, planes)
    def _(step):
        pl.semaphore_signal(
            barrier,
            inc=1,
            device_id=(me, other_plane(step)),
            device_id_type=pl.DeviceIdType.MESH,
        )

    @pl.loop(1, places)
    def _(step):
        pl.semaphore_signal(
            barrier,
            inc=1,
            device_id=(other_place(step), plane),
            device_id_type=pl.DeviceIdType.MESH,
        )

    pl.semaphore_wait(barrier, planes + places - 2)

    @pl.loop(1, planes)
    def _(step):
        target = other_plane(step)
        routing_copy(target, plane).start()
        column_copy(target, target, plane).start()

    routing[plane] = routing_ref[plane]
    column[plane] = normed_ref[...]
    answer_rows = normed_ref.shape[0]
    slots = lax.broadcasted_iota(jnp.int32, (capacity, answer_rows), 0).astype(jnp.float32)

    def dispatch(block):
        def rows_for(place):
            select = jnp.where(routing[block, place] == slots, 1.0, 0.0).astype(jnp.bfloat16)
            return jnp.dot(select, column[block], preferred_element_type=jnp.float32).astype(
                jnp.bfloat16
            )

        @pl.loop(1, places)
        def _(step):
            target = other_place(step)
            outbox[block, target] = rows_for(target)
            out_copy(block, target, me).start()

        inbox[block, me] = rows_for(me)

    dispatch(plane)

    @pl.loop(1, planes)
    def _(step):
        block = other_plane(planes - step)
        routing_copy(block, block).wait_recv()
        column_copy(block, block, block).wait_recv()
        dispatch(block)

    @pl.loop(1, planes + 1)
    def _(step):
        block = other_plane(planes - lax.rem(step, planes))

        @pl.loop(1, places)
        def _(turn):
            owner = other_place(turn)
            out_copy(block, owner, owner).wait_recv()

        rows = inbox[block].reshape(places * capacity, model_width)
        gate_part = jnp.dot(rows, gate_ref[...], preferred_element_type=jnp.float32)
        up_part = jnp.dot(rows, up_ref[...], preferred_element_type=jnp.float32)
        activated = (gate_part / (1.0 + jnp.exp(-gate_part)) * up_part).astype(jnp.bfloat16)
        inbox[block] = (
            jnp.dot(activated, down_ref[...], preferred_element_type=jnp.float32)
            .astype(jnp.bfloat16)
            .reshape(places, capacity, model_width)
        )

        @pl.loop(1, places)
        def _(turn):
            back_copy(block, other_place(turn), me).start()

        returned[block, me] = inbox[block, me]

    def combined(block):
        @pl.loop(1, places)
        def _(turn):
            owner = other_place(turn)
            back_copy(block, owner, owner).wait_recv()

        shares = jnp.concatenate(
            [
                jnp.where(routing[block, place] == slots, routing[block, places + place], 0.0)
                for place in range(places)
            ],
            axis=0,
        )
        return jnp.dot(
            shares.T.astype(jnp.bfloat16),
            returned[block].reshape(places * capacity, model_width),
            preferred_element_type=jnp.float32,
        )

    @pl.loop(1, planes)
    def _(step):
        block = other_plane(planes - step)
        partial[block] = combined(block).astype(jnp.bfloat16)
        sum_copy(block, plane).start()

    total = residual_ref[...].astype(jnp.float32) + combined(plane)
    for step in range(1, planes):
        owner = other_plane(step)
        sum_copy(owner, owner).wait_recv()
        total = total + summed[owner].astype(jnp.float32)
    out_ref[...] = total.astype(jnp.bfloat16)

    @pl.loop(1, planes)
    def _(step):
        target = other_plane(step)
        routing_copy(target, plane).wait_send()
        column_copy(target, target, plane).wait_send()
        sum_copy(target, plane).wait_send()

    @pl.loop(0, planes)
    def _(block):
        @pl.loop(1, places)
        def _(turn):
            target = other_place(turn)
            out_copy(block, target, me).wait_send()
            back_copy(block, target, me).wait_send()


def mix_experts(residual, normed, routing, capacity, gate_matrix, up_matrix, down_matrix):
    planes, places = routing.shape[0], routing.shape[1] // 2
    answer_rows, model_width = normed.shape
    box = pltpu.VMEM((planes, places, capacity, model_width), jnp.bfloat16)
    blocks = pltpu.VMEM((planes, answer_rows, model_width), jnp.bfloat16)
    per_plane = pltpu.SemaphoreType.DMA((planes,))
    per_pair = pltpu.SemaphoreType.DMA((planes, places))
    return pl.pallas_call(
        experts_kernel,
        out_shape=jax.ShapeDtypeStruct(residual.shape, jnp.bfloat16),
        in_specs=[pl.BlockSpec(memory_space=pltpu.VMEM)] * 6,
        out_specs=pl.BlockSpec(memory_space=pltpu.VMEM),
        scratch_shapes=[pltpu.VMEM(routing.shape, jnp.float32)]
        + [blocks, box, box, box, blocks, blocks]
        + [per_plane, per_plane, per_plane, per_plane, per_pair, per_pair, per_pair, per_pair, per_plane, per_plane],
        compiler_params=pltpu.CompilerParams(
            collective_id=0, has_side_effects=True, vmem_limit_bytes=60 * 2**20
        ),
        cost_estimate=pl.CostEstimate(
            flops=6 * planes * places * capacity * gate_matrix.size,
            bytes_accessed=6 * gate_matrix.size,
            transcendentals=0,
        ),
        name="mix_experts",
    )(residual, normed, routing, gate_matrix, up_matrix, down_matrix)


def on_device(
    hidden,
    queries,
    new_keys,
    new_values,
    cache_keys,
    cache_values,
    option_ids,
    prompt_lengths,
    query_gain,
    key_gain,
    out_proj,
    post_gain,
    route_ids,
    route_weights,
    expert_gate,
    expert_up,
    expert_down,
):
    answer_rows, model_width = hidden.shape
    top_count = route_ids.shape[1]
    attn_count = lax.axis_size("attn")
    expert_count = lax.axis_size("expert")
    device_count = attn_count * expert_count
    capacity = 3 * answer_rows * top_count // (2 * device_count)
    capacity = (capacity + 15) // 16 * 16

    gate_share = route_weights / jnp.sum(route_weights, axis=1, keepdims=True)
    experts = jnp.arange(device_count, dtype=jnp.int32).reshape(attn_count, expert_count).T
    chosen = route_ids[None, None, :, :] == experts[:, :, None, None]
    share = jnp.sum(jnp.where(chosen, gate_share[None, None, :, :], 0.0), axis=-1)
    hit = jnp.any(chosen, axis=-1)
    positions = jnp.arange(answer_rows)
    earlier = (positions[:, None] < positions[None, :]).astype(jnp.bfloat16)
    rank = jnp.einsum(
        "ear,rs->eas", hit.astype(jnp.bfloat16), earlier, preferred_element_type=jnp.float32
    )
    slot = jnp.where(hit, rank, -1.0)
    routing = jnp.concatenate([slot, share], axis=1)[:, :, None, :]

    attended = attend(
        queries,
        new_keys,
        new_values,
        cache_keys[0],
        cache_values[0],
        option_ids,
        prompt_lengths,
        query_gain,
        key_gain,
    )
    swapped = lax.all_to_all(attended, "expert", split_axis=1, concat_axis=0, tiled=True)
    projected = lax.psum_scatter(
        jnp.dot(swapped, out_proj, preferred_element_type=jnp.float32).astype(jnp.bfloat16),
        "expert",
        scatter_dimension=0,
        tiled=True,
    ).astype(jnp.float32)
    residual = (hidden.astype(jnp.float32) + projected).astype(jnp.bfloat16)
    normed = rms_scaled(residual.astype(jnp.float32), post_gain).astype(jnp.bfloat16)

    return mix_experts(
        residual,
        normed,
        routing,
        capacity,
        expert_gate[0],
        expert_up[0],
        expert_down[0],
    )


def solution(mesh):
    rows = P(("attn", "expert"), None)
    blocks = P(("attn", "expert"), None, None)
    placed = (
        rows,
        rows,
        rows,
        rows,
        blocks,
        blocks,
        rows,
        P(("attn", "expert")),
        P(),
        P(),
        P("expert", None),
        P(),
        rows,
        rows,
        blocks,
        blocks,
        blocks,
    )
    return jax.shard_map(
        on_device,
        mesh=mesh,
        in_specs=placed,
        out_specs=rows,
        check_vma=False,
    )
```
